32 devices in a mesh: grp: 2 (over x), gx: 16 (over z, y, core).
Axes of the slice: x: 2, y: 2, z: 4, core: 2. Of those that a mesh axis runs over, the one named last changes fastest.
Arguments:
- hidden_state: bfloat16 [32, 16384], P('grp', 'gx'), parts along dimension 0, may hold values from -120 to 120
- norm_gain: bfloat16 [16384], P('gx'), may hold values from 0.099609375 to 1.8984375
- w_query: bfloat16 [16384, 16384], P('gx'), may hold values from -0.0625 to 0.0625
- w_key: bfloat16 [16384, 1024], P('gx'), may hold values from -0.046875 to 0.046875
- w_value: bfloat16 [16384, 1024], P('gx'), may hold values from -0.046875 to 0.046875
- w_out: bfloat16 [16384, 16384], P(None, 'gx'), may hold values from -0.25 to 0.25
- cache_keys: bfloat16 [32, 512, 1024], P('grp', 'gx'), parts along dimension 0, may hold values from -384 to 384
- cache_values: bfloat16 [32, 512, 1024], P('grp', 'gx'), parts along dimension 0, may hold values from -6 to 6
- lengths: int32 [32], P('grp'), parts along dimension 0, may hold values from 1 to 512, 4096 in all
Outputs:
- attention_out: bfloat16 [32, 16384], P('grp', 'gx'), parts along dimension 0
- new_entries: bfloat16 [2, 32, 1024], P(None, 'grp'), parts along dimension 1
The draws below stay inside these ranges and needn't reach their ends.
There are 2 independent parts, one for each index of `grp`. The reference program is written for one: setup_inputs(seed, part) draws one part's arguments, and reference() takes and returns one part's arrays. A program takes and returns all parts, laid end to end along the dimension named above; an argument that names none is the same for every part. Nothing has to cross between parts.
All inputs are finite; a program needn't handle non-finite values.
Results may differ from the reference program's by a relative error of at most 0.004.
The reference program's roundings to bfloat16 on the way count: a program that leaves them out, or rounds other values in their place, can miss the bound.
Values may be sent and summed in bfloat16 or wider, within the bound.
A program may use at most 192 MiB of HBM per device.

```python
import math
import jax
import jax.numpy as jnp
import numpy as np
from jax import lax

D = 16384
H = 128
KV = 8
HD = 128
ROWS = 16
POS_DEV = 32
CTX = 512
N_GX = 16


def draw_hidden_state(key, part):
    key = jax.random.fold_in(key, 11)
    base_key, column_key = jax.random.split(key, 2)
    ramp = 1.0 + 2.0 * jnp.arange(D, dtype=jnp.float32) / D
    column_scale = ramp * jnp.exp(jax.random.uniform(column_key, (D,), jnp.float32, -0.7, 0.7))
    base_part = jnp.clip(jax.random.normal(base_key, (ROWS, D), jnp.float32), -5.0, 5.0)
    return (base_part * column_scale[None, :]).astype(jnp.bfloat16)


def draw_cache_keys(key, part):
    key = jax.random.fold_in(key, 23)
    base_key = jax.random.fold_in(key, 0)
    base_part = jnp.clip(jax.random.normal(base_key, (ROWS, CTX, KV * HD), jnp.float32), -6.0, 6.0)
    return (2.5 * base_part).astype(jnp.bfloat16)


def strengthened(array, own_key, source, target, shards_of, factor):
    def block_of(position):
        return (jnp.arange(array.shape[position]) // (array.shape[position] // shards_of)).reshape((-1,) + (1,) * (array.ndim - 1 - position))

    one_side = jax.random.permutation(own_key, shards_of)[block_of(target)]
    far = (block_of(target) + shards_of // 2) % shards_of
    return jnp.where((block_of(source) == one_side) | (block_of(source) == far), factor * array, array)


def levels(own_key, shape, pieces, smallest, high):
    loudness, own = 1.0, jax.random.fold_in(own_key, 6)
    for axis_at, parts in pieces:
        draws = jnp.exp(jax.random.uniform(jax.random.fold_in(own, axis_at), (parts,), jnp.float32, smallest / len(pieces), high / len(pieces)))
        loudness = loudness * jnp.repeat(draws, shape[axis_at] // parts).reshape([-1 if axis == axis_at else 1 for axis in range(len(shape))])
    return loudness


def split_up(number_of, total, bound, lean):
    loads = [(1 << 20) // math.isqrt(rank ** lean) + 1 for rank in range(2, number_of + 1)]
    spare, given = total - bound - (number_of - 1), [1] * (number_of - 1)
    while spare > 0:
        movable = [i for i in range(number_of - 1) if given[i] < bound]
        whole, remaining = sum([loads[i] for i in movable]), spare
        for i in movable:
            more = min(bound - given[i], max(1, remaining * loads[i] // whole), spare)
            given[i] = given[i] + more
            spare = spare - more
    return np.array([bound] + given)


def ragged_sizes(key, amount, total, most, skew):
    if amount == 2:
        one = jax.random.randint(key, (), max(1, total - most), min(most, total - 1) + 1)
        return jnp.stack([one, total - one])
    sizes = jnp.asarray(split_up(amount, total, most, skew), jnp.int32)
    pairs = (amount - 1) // 2
    giver, sink = sizes[1:1 + 2 * pairs:2], sizes[2:2 + 2 * pairs:2]
    margin = jnp.minimum(giver - 1, most - sink)
    shifted = jax.random.randint(jax.random.fold_in(key, 1), (pairs,), 0, 1 << 20) % (margin + 1)
    sizes = sizes.at[1:1 + 2 * pairs:2].set(giver - shifted).at[2:2 + 2 * pairs:2].set(sink + shifted)
    return sizes[jax.random.permutation(jax.random.fold_in(key, 2), amount)]


def centred(rng, extent, spread, limit, cuts=(), held_as=jnp.bfloat16):
    result = jax.random.normal(rng, extent, jnp.float32) * spread
    if len(cuts) > 0:
        result = levels(rng, extent, cuts, -0.22, 0.18) * result
    return jnp.clip(result, min=-limit, max=limit).astype(held_as)


def noise_with(stream_key, shape, deviation, most, cuts, heavy, kind=jnp.bfloat16):
    array = deviation * jax.random.normal(stream_key, shape, jnp.float32)
    if cuts:
        array = array * levels(stream_key, shape, cuts, -0.22, 0.18)
    return jnp.clip(strengthened(array, jax.random.fold_in(stream_key, 3), *heavy), -most, most).astype(kind)


def setup_inputs(seed: int = 0, part: int = 0) -> dict:
    keys = jax.random.split(jax.random.key(seed), 10)
    part_keys = jax.random.split(jax.random.fold_in(keys[9], part), 10)
    hidden_state = draw_hidden_state(jax.random.fold_in(jax.random.fold_in(keys[9], part), 71), part)
    norm_gain = jnp.clip(1.0 + 0.18 * jax.random.normal(keys[1], (D,), jnp.float32), 0.099609375, 1.8984375).astype(jnp.bfloat16)
    w_query = noise_with(keys[2], (D, H * HD), D ** -0.5, 0.0625, ((0, 16),), (0, 1, 16, 2.0))
    w_key = centred(keys[3], (D, KV * HD), D ** -0.5, 0.046875, ((0, 16),))
    w_value = centred(keys[4], (D, KV * HD), D ** -0.5, 0.046875, ((0, 16),))
    w_out = noise_with(keys[5], (H * HD, D), (H * HD // 16) ** -0.5, 0.25, ((1, 16),), (0, 1, 16, 2.0))
    cache_keys = draw_cache_keys(jax.random.fold_in(jax.random.fold_in(keys[9], part), 71), part)
    cache_values = centred(part_keys[7], (ROWS, CTX, KV * HD), 1.0, 6.0, ((1, 16),))
    lengths = ragged_sizes(part_keys[8], ROWS, ROWS * POS_DEV * N_GX // 2, POS_DEV * N_GX, 1).astype(jnp.int32)
    return {"hidden_state": hidden_state, "norm_gain": norm_gain, "w_query": w_query, "w_key": w_key, "w_value": w_value, "w_out": w_out, "cache_keys": cache_keys, "cache_values": cache_values, "lengths": lengths}


EPS = 1e-05
BASE = 500000.0

def rotate(values, positions):
    row_count = values.shape[0]
    head_count = values.shape[1] // HD
    half_dim = HD // 2
    shaped = values.reshape(row_count, head_count, HD)
    frequency = jnp.exp(jnp.arange(half_dim, dtype=jnp.float32) * (-2.0 * math.log(BASE) / HD))
    angles = positions.astype(jnp.float32)[:, None, None] * frequency[None, None, :]
    cos_table = jnp.cos(angles)
    sin_table = jnp.sin(angles)
    leading = shaped[:, :, :half_dim]
    trailing = shaped[:, :, half_dim:]
    turned = jnp.concatenate([leading * cos_table - trailing * sin_table, trailing * cos_table + leading * sin_table], axis=-1)
    return turned.reshape(row_count, head_count * HD)

def attend_row(inputs):
    query_row, key_rows, value_rows, new_key_row, new_value_row, length_row = inputs
    group_size = H // KV
    block_count = CTX // POS_DEV
    scale_factor = HD ** (-0.5)
    queries = query_row.astype(jnp.float32).reshape(KV, group_size, HD)
    key_block = key_rows.astype(jnp.float32).reshape(CTX, KV, HD)
    value_block = value_rows.astype(jnp.float32).reshape(block_count, POS_DEV, KV, HD)
    scores = jnp.einsum('kgd,tkd->kgt', queries, key_block) * scale_factor
    valid_mask = (jnp.arange(CTX) < length_row).reshape(block_count, POS_DEV)
    scores = scores.reshape(KV, group_size, block_count, POS_DEV)
    scores = jnp.where(valid_mask[None, None, :, :], scores, -1e+30)
    block_peak = lax.optimization_barrier(jnp.max(scores, axis=3))
    weights = jnp.where(valid_mask[None, None, :, :], jnp.exp(scores - block_peak[:, :, :, None]), 0.0)
    block_total = lax.optimization_barrier(jnp.sum(weights, axis=3))
    rounded = lax.optimization_barrier(weights.astype(jnp.bfloat16)).astype(jnp.float32)
    block_mix = jnp.einsum('kgjt,jtkd->kgjd', rounded, value_block)
    own_score = jnp.einsum('kgd,kd->kg', queries, new_key_row.astype(jnp.float32).reshape(KV, HD)) * scale_factor
    peak_score = jnp.maximum(lax.optimization_barrier(jnp.max(block_peak, axis=2)), own_score)
    rescale = jnp.exp(block_peak - peak_score[:, :, None])
    own_weight = jnp.exp(own_score - peak_score)
    total_weight = lax.optimization_barrier(jnp.sum(rescale * block_total, axis=2)) + own_weight
    own_value = new_value_row.astype(jnp.float32).reshape(KV, 1, HD)
    mixed = jnp.einsum('kgj,kgjd->kgd', rescale, block_mix) + own_weight[:, :, None] * own_value
    head_out = mixed / total_weight[:, :, None]
    return head_out.reshape(H * HD).astype(jnp.bfloat16)

def reference(hidden_state, norm_gain, w_query, w_key, w_value, w_out, cache_keys, cache_values, lengths):
    widened = hidden_state.astype(jnp.float32)
    sum_sq = lax.optimization_barrier(jnp.sum(widened * widened, axis=1))
    scaled = (widened * norm_gain.astype(jnp.float32)[None, :]).astype(jnp.bfloat16)
    inv_rms = lax.rsqrt(sum_sq / D + EPS)[:, None]
    query_raw = inv_rms * jnp.dot(scaled, w_query, preferred_element_type=jnp.float32)
    key_raw = inv_rms * jnp.dot(scaled, w_key, preferred_element_type=jnp.float32)
    value_raw = inv_rms * jnp.dot(scaled, w_value, preferred_element_type=jnp.float32)
    queries = rotate(query_raw, lengths).astype(jnp.bfloat16)
    new_key = rotate(key_raw, lengths).astype(jnp.bfloat16)
    new_value = value_raw.astype(jnp.bfloat16)
    head_out = lax.map(attend_row, (queries, cache_keys, cache_values, new_key, new_value, lengths))
    attention_out = jnp.dot(head_out, w_out, preferred_element_type=jnp.float32).astype(jnp.bfloat16)
    return (attention_out, jnp.stack([new_key, new_value]))
```

```python
import functools
import math

import jax
import jax.numpy as jnp
from jax import lax
from jax.experimental import pallas as pl
from jax.experimental.pallas import tpu as pltpu
from jax.sharding import PartitionSpec as P

HD = 128
EPS = 1e-05
BASE = 500000.0
SLOTS = 4
F32 = jnp.float32
BF16 = jnp.bfloat16


def kernel(
    n, hidden, gain, cos_ref, sin_ref, limit, wq, wk, wv, wo, ck, cv,
    out, new,
    wbuf, kvbuf, wobuf, ckb, cvb, kvp, part, sibr, dirr, qg, mixb, sibm, mixs, stats, mixr, statr,
    hacc, hg, acc,
    wsem, kvsem, wosem, csem, s1s, s1r, d1s, d1r, g1s, g1r, r1s, r1r, s2s, s2r, d2s, d2r, t2s, t2r,
    g2s, g2r, r2s, r2r,
):
    rows, depth = hidden.shape
    width = wbuf.shape[2]
    local = width // HD
    kv = ck.shape[1] // HD
    group = n * local // kv
    chips = n // 2
    per_kv = group // local
    chips_kv = per_kv // 2
    kv_devs = n // (2 * kv)
    spots = ck.shape[0] // rows
    me = lax.axis_index("gx")
    core = lax.rem(me, 2)
    chip = me // 2
    other = 1 - core
    sibling = 2 * chip + other

    def turn(index):
        return lax.rem(index + 2 * chips, chips)

    def remote(src, dst, send, recv, target):
        return pltpu.make_async_remote_copy(
            src_ref=src, dst_ref=dst, send_sem=send, recv_sem=recv,
            device_id={"gx": target}, device_id_type=pl.DeviceIdType.MESH,
        )

    def each_other(body):
        def step(u, carry):
            body(u)
            return carry
        lax.fori_loop(1, chips, step, 0)

    barrier = pltpu.get_barrier_semaphore()
    pl.semaphore_signal(barrier, inc=1, device_id={"gx": sibling}, device_id_type=pl.DeviceIdType.MESH)
    each_other(lambda u: pl.semaphore_signal(
        barrier, inc=1, device_id={"gx": 2 * turn(chip + u) + core}, device_id_type=pl.DeviceIdType.MESH))

    def load_w(t, second):
        c = turn(chip + 1 + t)
        d = 2 * c + (core if second else other)
        slot = lax.rem(2 * t + second, SLOTS)
        return pltpu.make_async_copy(
            wq.at[:, pl.ds(pl.multiple_of(d * width, HD), width)], wbuf.at[slot], wsem.at[slot])

    copy_k = pltpu.make_async_copy(wk, kvbuf.at[0], kvsem.at[0])
    copy_v = pltpu.make_async_copy(wv, kvbuf.at[1], kvsem.at[1])
    copy_k.start()
    copy_v.start()
    for t in range(SLOTS // 2):
        load_w(t, 0).start()
        load_w(t, 1).start()

    wide = hidden[...].astype(F32)
    squares = jnp.broadcast_to(jnp.sum(wide * wide, axis=1, keepdims=True), (rows, HD))
    scaled = (wide * gain[...].astype(F32)).astype(BF16)
    kv_width = kv * HD
    copy_k.wait()
    kvp[:, :kv_width] = jnp.dot(scaled, kvbuf[0], preferred_element_type=F32)
    copy_v.wait()
    kvp[:, kv_width:] = jnp.dot(scaled, kvbuf[1], preferred_element_type=F32)

    pl.semaphore_wait(barrier, chips)

    def sib1(c):
        return remote(part.at[2 * c + other], sibr.at[c], s1s.at[c], s1r.at[c], sibling)

    def dir1(c):
        return remote(part.at[2 * c + core], dirr.at[chip], d1s.at[c], d1r.at[chip], 2 * c + core)

    def dir1_in(c):
        return remote(part.at[me], dirr.at[c], d1s.at[c], d1r.at[c], 2 * c + core)

    def finish1(c):
        sib1(c).wait_recv()
        d = 2 * c + core
        part[d] = part[d] + sibr[c]

    def project(t, carry):
        c = turn(chip + 1 + t)
        for second in range(2):
            d = 2 * c + (core if second else other)
            slot = lax.rem(2 * t + second, SLOTS)
            load_w(t, second).wait()
            part[d, :, :width] = jnp.dot(scaled, wbuf[slot], preferred_element_type=F32)
            start = pl.multiple_of((d // kv_devs) * HD, HD)
            part[d, :, width:width + HD] = kvp[:, pl.ds(start, HD)]
            part[d, :, width + HD:] = squares

            @pl.when(t + SLOTS // 2 < chips)
            def _():
                load_w(t + SLOTS // 2, second).start()

            if not second:
                sib1(c).start()

        @pl.when(t > 0)
        def _():
            before = turn(chip + t)
            finish1(before)
            dir1(before).start()

        return carry

    lax.fori_loop(0, chips, project, 0)

    copy_ck = pltpu.make_async_copy(ck, ckb, csem.at[0])
    copy_cv = pltpu.make_async_copy(cv, cvb, csem.at[1])
    copy_ck.start()
    copy_cv.start()

    def load_wo(d):
        return pltpu.make_async_copy(
            wo.at[pl.ds(pl.multiple_of(d * width, HD), width), :], wobuf.at[d], wosem.at[d])

    def start_wo(i, carry):
        c = turn(chip - i)
        load_wo(2 * c + core).start()
        load_wo(2 * c + other).start()
        return carry

    lax.fori_loop(0, chips, start_wo, 0)

    finish1(chip)

    def gather1(u):
        c = turn(chip - u)
        dir1_in(c).wait_recv()
        part[me] = part[me] + dirr[c]

    each_other(gather1)

    inv = lax.rsqrt(part[me, :, width + HD:] / (depth * n) + EPS)
    cos_table, sin_table = cos_ref[...], sin_ref[...]
    for j in range(local):
        x = part[me, :, j * HD:(j + 1) * HD] * inv
        qg[me, :, j * HD:(j + 1) * HD] = (x * cos_table + pltpu.roll(x, HD // 2, 1) * sin_table).astype(BF16)
    is_key = (me // kv_devs < kv).astype(F32)
    x = part[me, :, width:width + HD] * inv
    cos_key = cos_table * is_key + (1.0 - is_key)
    qg[me, :, width:] = (x * cos_key + pltpu.roll(x, HD // 2, 1) * (sin_table * is_key)).astype(BF16)

    def out1(c):
        return remote(qg.at[me], qg.at[me], g1s.at[c], g1r.at[chip], 2 * c + core)

    def in1(c):
        return remote(qg.at[2 * c + core], qg.at[2 * c + core], g1s.at[c], g1r.at[c], 2 * c + core)

    def rel1(c):
        return remote(qg.at[2 * c + core], qg.at[2 * c + core], r1s.at[c], r1r.at[c], sibling)

    def rel1_in(c):
        return remote(qg.at[2 * c + other], qg.at[2 * c + other], r1s.at[c], r1r.at[c], sibling)

    rel1(chip).start()
    each_other(lambda u: out1(turn(chip + u)).start())

    def chips_of(k, body):
        def step(i, carry):
            body(k * chips_kv + i)
            return carry
        lax.fori_loop(0, chips_kv, step, 0)

    def relay1(k):
        def one(c):
            @pl.when(c != chip)
            def _():
                in1(c).wait_recv()
                rel1(c).start()
        chips_of(k, one)

    column = lax.broadcasted_iota(jnp.int32, (group * rows, rows * spots), 1)
    row = lax.broadcasted_iota(jnp.int32, (group * rows, rows * spots), 0)
    valid = (lax.rem(row, rows) == column // spots) & (limit[...] > me * spots)
    lane = lax.broadcasted_iota(jnp.int32, (rows, HD), 1)
    half = HD // 2

    def sib2(c):
        return remote(mixb.at[2 * c + other], sibm.at[c], s2s.at[c], s2r.at[c], sibling)

    def dir2(c, slot):
        return remote(mixs.at[c], mixr.at[slot], d2s.at[c], d2r.at[slot], 2 * c + core)

    def dir2_stat(c, slot):
        return remote(stats.at[c], statr.at[slot], t2s.at[c], t2r.at[slot], 2 * c + core)

    def finish2(k):
        def one(c):
            sib2(c).wait_recv()
            d = 2 * c + core
            first, second = mixb[d, :, width:], sibm[c, :, width:]
            top = jnp.maximum(first, second)
            e_first, e_second = jnp.exp(first - top), jnp.exp(second - top)
            total = pltpu.roll(first, half, 1) * e_first + pltpu.roll(second, half, 1) * e_second
            stats[c] = jnp.where(lane < half, top, pltpu.roll(total, half, 1))
            for j in range(local):
                at = slice(j * HD, (j + 1) * HD)
                mixs[c, :, at] = (
                    e_first[:, j:j + 1] * mixb[d, :, at] + e_second[:, j:j + 1] * sibm[c, :, at]
                ).astype(BF16)

            @pl.when(c != chip)
            def _():
                dir2(c, chip).start()
                dir2_stat(c, chip).start()
        chips_of(k, one)

    first_kv = chip // chips_kv

    def kv_at(t):
        return lax.rem(first_kv - t + 2 * kv, kv)

    relay1(first_kv)
    copy_ck.wait()
    copy_cv.wait()

    def attend(t, carry):
        k = kv_at(t)

        @pl.when(t + 1 < kv)
        def _():
            relay1(kv_at(t + 1))

        chips_of(k, lambda c: rel1_in(c).wait_recv())
        query = jnp.concatenate(
            [qg[k * per_kv + h // local, :, (h % local) * HD:(h % local + 1) * HD] for h in range(group)], axis=0)
        at = pl.ds(pl.multiple_of(k * HD, HD), HD)
        scores = lax.dot_general(
            query, ckb[:, at], (((1,), (1,)), ((), ())), preferred_element_type=F32) * (HD ** -0.5)
        scores = jnp.where(valid, scores, -1e30)
        peak = jnp.max(scores, axis=1, keepdims=True)
        weights = jnp.where(valid, jnp.exp(scores - peak), 0.0)
        total = jnp.sum(weights, axis=1, keepdims=True)
        mix = jnp.dot(weights.astype(BF16), cvb[:, at], preferred_element_type=F32)
        for i in range(per_kv):
            d = k * per_kv + i
            stat = jnp.zeros((rows, HD), F32)
            for j in range(local):
                h = i * local + j
                here = slice(h * rows, (h + 1) * rows)
                mixb[d, :, j * HD:(j + 1) * HD] = mix[here]
                stat = jnp.where(lane == j, peak[here], stat)
                stat = jnp.where(lane == half + j, total[here], stat)
            mixb[d, :, width:] = stat
        chips_of(k, lambda c: sib2(c).start())

        @pl.when(t > 0)
        def _():
            finish2(kv_at(t - 1))

        return carry

    lax.fori_loop(0, kv, attend, 0)
    finish2(kv_at(kv - 1))

    for i in range(kv):
        new[0, :, i * HD:(i + 1) * HD] = qg[i * kv_devs, :, width:]
        new[1, :, i * HD:(i + 1) * HD] = qg[(kv + i) * kv_devs, :, width:]

    my_kv = me * local // group
    own_key = qg[my_kv * kv_devs, :, width:].astype(F32)
    own_value = qg[(kv + my_kv) * kv_devs, :, width:].astype(F32)
    own = jnp.zeros((rows, HD), F32)
    for j in range(local):
        score = jnp.sum(qg[me, :, j * HD:(j + 1) * HD].astype(F32) * own_key, axis=1, keepdims=True)
        own = jnp.where(lane == j, score * (HD ** -0.5), own)

    statr[chip] = stats[chip]
    mixr[chip] = mixs[chip]

    def peaks(u, top):
        c = turn(chip - u)
        dir2_stat(c, c).wait_recv()
        return jnp.maximum(top, statr[c])

    top = lax.fori_loop(1, chips, peaks, jnp.maximum(own, stats[chip]))
    own_weight = jnp.exp(own - top)
    for j in range(local):
        hacc[:, j * HD:(j + 1) * HD] = own_weight[:, j:j + 1] * own_value

    def add(c, total):
        stat = statr[c]
        scale = jnp.exp(stat - top)
        for j in range(local):
            at = slice(j * HD, (j + 1) * HD)
            hacc[:, at] = hacc[:, at] + scale[:, j:j + 1] * mixr[c, :, at].astype(F32)
        return total + scale * pltpu.roll(stat, half, 1)

    def add_other(u, total):
        c = turn(chip - u)
        dir2(c, c).wait_recv()
        return add(c, total)

    total = lax.fori_loop(1, chips, add_other, add(chip, own_weight))
    for j in range(local):
        at = slice(j * HD, (j + 1) * HD)
        hg[me, :, at] = (hacc[:, at] / total[:, j:j + 1]).astype(BF16)

    def out2(c):
        return remote(hg.at[me], hg.at[me], g2s.at[c], g2r.at[chip], 2 * c + core)

    def in2(c):
        return remote(hg.at[2 * c + core], hg.at[2 * c + core], g2s.at[c], g2r.at[c], 2 * c + core)

    def rel2(c):
        return remote(hg.at[2 * c + core], hg.at[2 * c + core], r2s.at[c], r2r.at[c], sibling)

    def rel2_in(c):
        return remote(hg.at[2 * c + other], hg.at[2 * c + other], r2s.at[c], r2r.at[c], sibling)

    rel2(chip).start()
    each_other(lambda u: out2(turn(chip + u)).start())

    def product(d):
        load_wo(d).wait()
        acc[...] = acc[...] + jnp.dot(hg[d], wobuf[d], preferred_element_type=F32)

    acc[...] = jnp.zeros_like(acc)
    product(me)

    def project_out(u):
        c = turn(chip - u)
        in2(c).wait_recv()
        rel2(c).start()
        before = turn(chip - u + 1)
        rel2_in(before).wait_recv()
        product(2 * before + other)
        product(2 * c + core)

    each_other(project_out)
    last = turn(chip + 1)
    rel2_in(last).wait_recv()
    product(2 * last + other)
    out[...] = acc[...].astype(BF16)

    def drain(c, carry):
        sib1(c).wait_send()
        rel1(c).wait_send()
        sib2(c).wait_send()
        rel2(c).wait_send()

        @pl.when(c != chip)
        def _():
            dir1(c).wait_send()
            out1(c).wait_send()
            dir2(c, chip).wait_send()
            dir2_stat(c, chip).wait_send()
            out2(c).wait_send()

        return carry

    lax.fori_loop(0, chips, drain, 0)


def on_device(hidden, norm_gain, w_query, w_key, w_value, w_out, cache_keys, cache_values, lengths):
    n = lax.axis_size("gx")
    rows, depth = hidden.shape
    spots, kv_width = cache_keys.shape[1:]
    width = w_query.shape[1] // n
    out_width = w_out.shape[1]
    chips = n // 2
    half = HD // 2
    frequency = jnp.exp(jnp.arange(half, dtype=F32) * (-2.0 * math.log(BASE) / HD))
    angles = lengths.astype(F32)[:, None] * frequency[None, :]
    cos_half, sin_half = jnp.cos(angles), jnp.sin(angles)
    cos_table = jnp.concatenate([cos_half, cos_half], axis=1)
    sin_table = jnp.concatenate([-sin_half, sin_half], axis=1)
    limit = (lengths[:, None] - jnp.arange(spots, dtype=jnp.int32)[None, :]).reshape(1, rows * spots)
    vmem = pl.BlockSpec(memory_space=pltpu.VMEM)
    hbm = pl.BlockSpec(memory_space=pl.ANY)
    dma = pltpu.SemaphoreType.DMA
    return pl.pallas_call(
        functools.partial(kernel, n),
        out_shape=(
            jax.ShapeDtypeStruct((rows, out_width), BF16),
            jax.ShapeDtypeStruct((2, rows, kv_width), BF16),
        ),
        in_specs=[vmem] * 5 + [hbm] * 6,
        out_specs=(vmem, vmem),
        scratch_shapes=[
            pltpu.VMEM((SLOTS, depth, width), BF16),
            pltpu.VMEM((2, depth, kv_width), BF16),
            pltpu.VMEM((n, width, out_width), BF16),
            pltpu.VMEM((rows * spots, kv_width), BF16),
            pltpu.VMEM((rows * spots, kv_width), BF16),
            pltpu.VMEM((rows, 2 * kv_width), F32),
            pltpu.VMEM((n, rows, width + 2 * HD), F32),
            pltpu.VMEM((chips, rows, width + 2 * HD), F32),
            pltpu.VMEM((chips, rows, width + 2 * HD), F32),
            pltpu.VMEM((n, rows, width + HD), BF16),
            pltpu.VMEM((n, rows, width + HD), F32),
            pltpu.VMEM((chips, rows, width + HD), F32),
            pltpu.VMEM((chips, rows, width), BF16),
            pltpu.VMEM((chips, rows, HD), F32),
            pltpu.VMEM((chips, rows, width), BF16),
            pltpu.VMEM((chips, rows, HD), F32),
            pltpu.VMEM((rows, width), F32),
            pltpu.VMEM((n, rows, width), BF16),
            pltpu.VMEM((rows, out_width), F32),
            dma((SLOTS,)), dma((2,)), dma((n,)), dma((2,)),
        ] + [dma((chips,)) for _ in range(18)],
        compiler_params=pltpu.CompilerParams(
            collective_id=0, has_side_effects=True, vmem_limit_bytes=60 * 1024 * 1024),
        cost_estimate=pl.CostEstimate(
            flops=4 * rows * depth * n * width, bytes_accessed=4 * depth * n * width, transcendentals=0),
    )(
        hidden, norm_gain.reshape(1, depth), cos_table, sin_table, limit, w_query, w_key, w_value, w_out,
        cache_keys.reshape(rows * spots, kv_width), cache_values.reshape(rows * spots, kv_width),
    )


def solution(mesh):
    return jax.shard_map(
        on_device,
        mesh=mesh,
        in_specs=(
            P("grp", "gx"),
            P("gx"),
            P("gx", None),
            P("gx", None),
            P("gx", None),
            P(None, "gx"),
            P("grp", "gx", None),
            P("grp", "gx", None),
            P("grp"),
        ),
        out_specs=(P("grp", "gx"), P(None, "grp", None)),
        check_vma=False,
    )
```

```python
import functools
import math

import jax
import jax.numpy as jnp
from jax import lax
from jax.experimental import pallas as pl
from jax.experimental.pallas import tpu as pltpu
from jax.sharding import PartitionSpec as P

HD = 128
EPS = 1e-05
BASE = 500000.0
AHEAD = 8
F32 = jnp.float32
BF16 = jnp.bfloat16


def kernel(
    n, hidden, gain, lengths, wq, wk, wv, wo, ck, cv,
    out, new,
    wbuf, kvbuf, ckb, cvb, kvp, part, sibr, yr, zr, qg, mixb, sibm, ym, zm, hacc, hg, acc,
    wsem, kvsem, wosem, csem, s1s, s1r, y1s, y1r, z1s, z1r, gss, gsr, gys, gyr, gzs, gzr,
    s2s, s2r, y2s, y2r, z2s, z2r, hss, hsr, hys, hyr, hzs, hzr,
):
    rows, depth = hidden.shape
    width = wbuf.shape[2]
    local = width // HD
    kv = ck.shape[1] // HD
    group = n * local // kv
    chips = n // 2
    pairs = chips // 2
    per_kv = group // local
    chips_kv = per_kv // 2
    kv_devs = n // (2 * kv)
    spots = ck.shape[0] // rows
    half = HD // 2
    me = lax.axis_index("gx")
    core = lax.rem(me, 2)
    chip = me // 2
    side = lax.rem(chip, 2)
    pair = chip // 2
    other = 1 - core
    sibling = 2 * chip + other
    across = 2 * (2 * pair + 1 - side) + core

    def turn(index):
        return lax.rem(index + 2 * pairs, pairs)

    def near(p):
        return 2 * p + side

    def far(p):
        return 2 * p + 1 - side

    def along(p):
        return 2 * near(p) + core

    def remote(src, dst, send, recv, target):
        return pltpu.make_async_remote_copy(
            src_ref=src, dst_ref=dst, send_sem=send, recv_sem=recv,
            device_id={"gx": target}, device_id_type=pl.DeviceIdType.MESH,
        )

    def each_other(body):
        def step(u, carry):
            body(turn(pair - u))
            return carry
        lax.fori_loop(1, pairs, step, 0)

    barrier = pltpu.get_barrier_semaphore()

    def greet(target):
        pl.semaphore_signal(barrier, inc=1, device_id={"gx": target}, device_id_type=pl.DeviceIdType.MESH)

    greet(sibling)
    greet(across)
    each_other(lambda p: greet(along(p)))

    def block(t, second):
        c = 2 * turn(pair + 1 + t // 2) + lax.rem(side + 1 + t, 2)
        return c, 2 * c + (core if second else other)

    def load_w(t, second):
        d = block(t, second)[1]
        return pltpu.make_async_copy(
            wq.at[:, pl.ds(pl.multiple_of(d * width, HD), width)], wbuf.at[d], wsem.at[d])

    copy_k = pltpu.make_async_copy(wk, kvbuf.at[0], kvsem.at[0])
    copy_v = pltpu.make_async_copy(wv, kvbuf.at[1], kvsem.at[1])
    copy_k.start()
    copy_v.start()
    for t in range(AHEAD // 2):
        load_w(t, 0).start()
        load_w(t, 1).start()

    row_at = lax.broadcasted_iota(jnp.int32, (rows, HD), 0)
    lane = lax.broadcasted_iota(jnp.int32, (rows, HD), 1)
    owner_row = lax.broadcasted_iota(jnp.int32, (1, rows * spots), 1)
    by_row = jnp.zeros((rows, HD), jnp.int32)
    by_column = jnp.zeros((1, rows * spots), jnp.int32)
    for r in range(rows):
        size = lengths[r]
        by_row = jnp.where(row_at == r, size, by_row)
        by_column = jnp.where(owner_row // spots == r, size, by_column)
    limit = by_column - lax.rem(owner_row, spots)
    frequency = jnp.exp(lax.rem(lane, half).astype(F32) * (-2.0 * math.log(BASE) / HD))
    angles = by_row.astype(F32) * frequency
    cos_table = jnp.cos(angles)
    sin_table = jnp.sin(angles)
    sin_table = jnp.where(lane < half, -sin_table, sin_table)

    wide = hidden[...].astype(F32)
    squares = jnp.broadcast_to(jnp.sum(wide * wide, axis=1, keepdims=True), (rows, HD))
    scaled = (wide * gain[...].astype(F32)[None, :]).astype(BF16)
    kv_width = kv * HD
    copy_k.wait()
    kvp[:, :kv_width] = jnp.dot(scaled, kvbuf[0], preferred_element_type=F32)
    copy_v.wait()
    kvp[:, kv_width:] = jnp.dot(scaled, kvbuf[1], preferred_element_type=F32)

    pl.semaphore_wait(barrier, pairs + 1)

    def sib1(c):
        return remote(part.at[2 * c + other], sibr.at[c], s1s.at[c], s1r.at[c], sibling)

    def y1(p):
        return remote(part.at[2 * far(p) + core], yr.at[p], y1s.at[p], y1r.at[p], across)

    def z1(p):
        return remote(part.at[along(p)], zr.at[pair], z1s.at[p], z1r.at[pair], along(p))

    def z1_in(p):
        return remote(part.at[me], zr.at[p], z1s.at[p], z1r.at[p], along(p))

    def finish1_far(p):
        c = far(p)
        sib1(c).wait_recv()
        part[2 * c + core] = part[2 * c + core] + sibr[c]
        y1(p).start()

    def finish1_near(p):
        c = near(p)
        sib1(c).wait_recv()
        y1(p).wait_recv()
        part[2 * c + core] = part[2 * c + core] + sibr[c] + yr[p]

    def project_side(i, is_near):
        t = 2 * i + is_near
        for second in range(2):
            c, d = block(t, second)
            load_w(t, second).wait()
            part[d, :, :width] = jnp.dot(scaled, wbuf[d], preferred_element_type=F32)
            start = pl.multiple_of((d // kv_devs) * HD, HD)
            part[d, :, width:width + HD] = kvp[:, pl.ds(start, HD)]
            part[d, :, width + HD:] = squares

            @pl.when(t + AHEAD // 2 < chips)
            def _():
                load_w(t + AHEAD // 2, second).start()

            if not second:
                sib1(c).start()

    def project(i, carry):
        project_side(i, 0)

        @pl.when(i > 0)
        def _():
            before = turn(pair + i)
            finish1_near(before)
            z1(before).start()

        project_side(i, 1)
        finish1_far(turn(pair + 1 + i))
        return carry

    lax.fori_loop(0, pairs, project, 0)

    copy_ck = pltpu.make_async_copy(ck, ckb, csem.at[0])
    copy_cv = pltpu.make_async_copy(cv, cvb, csem.at[1])
    copy_ck.start()
    copy_cv.start()

    def load_wo(d):
        return pltpu.make_async_copy(
            wo.at[pl.ds(pl.multiple_of(d * width, HD), width), :], wbuf.at[d], wosem.at[d])

    def start_wo(i, carry):
        p = turn(pair - i)
        for c in (near(p), far(p)):
            load_wo(2 * c + core).start()
            load_wo(2 * c + other).start()
        return carry

    lax.fori_loop(0, pairs, start_wo, 0)

    finish1_near(pair)

    def gather1(p):
        z1_in(p).wait_recv()
        part[me] = part[me] + zr[p]

    each_other(gather1)

    inv = lax.rsqrt(part[me, :, width + HD:] / (depth * n) + EPS)
    for j in range(local):
        x = part[me, :, j * HD:(j + 1) * HD] * inv
        qg[me, :, j * HD:(j + 1) * HD] = (x * cos_table + pltpu.roll(x, half, 1) * sin_table).astype(BF16)
    is_key = (me // kv_devs < kv).astype(F32)
    x = part[me, :, width:width + HD] * inv
    cos_key = cos_table * is_key + (1.0 - is_key)
    qg[me, :, width:] = (x * cos_key + pltpu.roll(x, half, 1) * (sin_table * is_key)).astype(BF16)

    class Spread:
        def __init__(self, ref, ss, sr, ys, yr_, zs, zr_):
            self.ref, self.sems = ref, (ss, sr, ys, yr_, zs, zr_)

        def to_sibling(self, c):
            ss, sr = self.sems[:2]
            at = self.ref.at[2 * c + core]
            return remote(at, at, ss.at[c], sr.at[c], sibling)

        def from_sibling(self, c):
            ss, sr = self.sems[:2]
            at = self.ref.at[2 * c + other]
            return remote(at, at, ss.at[c], sr.at[c], sibling)

        def to_across(self, p):
            ys, yr_ = self.sems[2:4]
            at = self.ref.at[along(p)]
            return remote(at, at, ys.at[p], yr_.at[p], across)

        def from_across(self, p):
            ys, yr_ = self.sems[2:4]
            at = self.ref.at[2 * far(p) + core]
            return remote(at, at, ys.at[p], yr_.at[p], across)

        def to_along(self, p):
            zs, zr_ = self.sems[4:]
            at = self.ref.at[me]
            return remote(at, at, zs.at[p], zr_.at[pair], along(p))

        def from_along(self, p):
            zs, zr_ = self.sems[4:]
            at = self.ref.at[along(p)]
            return remote(at, at, zs.at[p], zr_.at[p], along(p))

        def begin(self):
            def send(u, carry):
                self.to_along(turn(pair + u)).start()
                return carry
            lax.fori_loop(1, pairs, send, 0)
            self.to_across(pair).start()
            self.to_sibling(chip).start()

        def relay_near(self, p):
            self.from_along(p).wait_recv()
            self.to_across(p).start()
            self.to_sibling(near(p)).start()

        def relay_far(self, p):
            self.from_across(p).wait_recv()
            self.to_sibling(far(p)).start()

    spread1 = Spread(qg, gss, gsr, gys, gyr, gzs, gzr)
    spread1.begin()

    column = lax.broadcasted_iota(jnp.int32, (group * rows, rows * spots), 1)
    row = lax.broadcasted_iota(jnp.int32, (group * rows, rows * spots), 0)
    valid = (lax.rem(row, rows) == column // spots) & (limit > me * spots)

    def sib2(c):
        return remote(mixb.at[2 * c + other], sibm.at[c], s2s.at[c], s2r.at[c], sibling)

    def y2(p):
        return remote(mixb.at[2 * far(p) + core], ym.at[p], y2s.at[p], y2r.at[p], across)

    def z2(p):
        return remote(mixb.at[along(p)], zm.at[pair], z2s.at[p], z2r.at[pair], along(p))

    def z2_in(p):
        return remote(mixb.at[me], zm.at[p], z2s.at[p], z2r.at[p], along(p))

    def merge(d, from_ref, index):
        first, second = mixb[d, :, width:], from_ref[index, :, width:]
        top = jnp.maximum(first, second)
        e_first, e_second = jnp.exp(first - top), jnp.exp(second - top)
        total = pltpu.roll(first, half, 1) * e_first + pltpu.roll(second, half, 1) * e_second
        mixb[d, :, width:] = jnp.where(lane < half, top, pltpu.roll(total, half, 1))
        for j in range(local):
            at = slice(j * HD, (j + 1) * HD)
            mixb[d, :, at] = e_first[:, j:j + 1] * mixb[d, :, at] + e_second[:, j:j + 1] * from_ref[index, :, at]

    def finish2_far(p):
        c = far(p)
        sib2(c).wait_recv()
        merge(2 * c + core, sibm, c)
        y2(p).start()

    def finish2_near(p):
        c = near(p)
        sib2(c).wait_recv()
        merge(2 * c + core, sibm, c)
        y2(p).wait_recv()
        merge(2 * c + core, ym, p)

        @pl.when(p != pair)
        def _():
            z2(p).start()

    def attend(k):
        query = jnp.concatenate(
            [qg[k * per_kv + h // local, :, (h % local) * HD:(h % local + 1) * HD] for h in range(group)], axis=0)
        at = pl.ds(pl.multiple_of(k * HD, HD), HD)
        scores = lax.dot_general(
            query, ckb[:, at], (((1,), (1,)), ((), ())), preferred_element_type=F32) * (HD ** -0.5)
        scores = jnp.where(valid, scores, -1e30)
        peak = jnp.max(scores, axis=1, keepdims=True)
        weights = jnp.where(valid, jnp.exp(scores - peak), 0.0)
        total = jnp.sum(weights, axis=1, keepdims=True)
        mix = jnp.dot(weights.astype(BF16), cvb[:, at], preferred_element_type=F32)
        for i in range(per_kv):
            d = k * per_kv + i
            stat = jnp.zeros((rows, HD), F32)
            for j in range(local):
                h = i * local + j
                here = slice(h * rows, (h + 1) * rows)
                mixb[d, :, j * HD:(j + 1) * HD] = mix[here]
                stat = jnp.where(lane == j, peak[here], stat)
                stat = jnp.where(lane == half + j, total[here], stat)
            mixb[d, :, width:] = stat

        def send(i, carry):
            sib2(k * chips_kv + i).start()
            return carry

        lax.fori_loop(0, chips_kv, send, 0)

    if chips_kv == 1:
        copy_ck.wait()
        copy_cv.wait()
        spread1.from_sibling(chip).wait_recv()
        attend(chip)
        spread1.relay_far(pair)
        spread1.relay_near(turn(pair - 1))
        spread1.from_sibling(far(pair)).wait_recv()
        attend(far(pair))

        def of_pair(u, carry):
            p = turn(pair - u)
            spread1.relay_far(p)

            @pl.when(u + 1 < pairs)
            def _():
                spread1.relay_near(turn(pair - u - 1))

            spread1.from_sibling(far(p)).wait_recv()
            attend(far(p))
            finish2_far(turn(p + 1))
            spread1.from_sibling(near(p)).wait_recv()
            attend(near(p))

            @pl.when(u > 1)
            def _():
                finish2_near(turn(p + 1))

            return carry

        lax.fori_loop(1, pairs, of_pair, 0)
        last = turn(pair + 1)
        finish2_far(last)
        finish2_near(last)
        finish2_near(pair)
    else:
        each_other(spread1.relay_near)
        spread1.relay_far(pair)
        each_other(spread1.relay_far)
        copy_ck.wait()
        copy_cv.wait()

        def wait_chip(c, carry):
            spread1.from_sibling(c).wait_recv()
            return carry

        lax.fori_loop(0, chips, wait_chip, 0)

        def of_kv(k, carry):
            attend(k)

            def finish_far(i, inner):
                finish2_far(k * chips_kv // 2 + i)
                return inner

            def finish_near(i, inner):
                finish2_near(k * chips_kv // 2 + i)
                return inner

            lax.fori_loop(0, chips_kv // 2, finish_far, 0)
            lax.fori_loop(0, chips_kv // 2, finish_near, 0)
            return carry

        lax.fori_loop(0, kv, of_kv, 0)

    for i in range(kv):
        new[0, :, i * HD:(i + 1) * HD] = qg[i * kv_devs, :, width:]
        new[1, :, i * HD:(i + 1) * HD] = qg[(kv + i) * kv_devs, :, width:]

    my_kv = me * local // group
    own_key = qg[my_kv * kv_devs, :, width:].astype(F32)
    own_value = qg[(kv + my_kv) * kv_devs, :, width:].astype(F32)
    own = jnp.zeros((rows, HD), F32)
    for j in range(local):
        score = jnp.sum(qg[me, :, j * HD:(j + 1) * HD].astype(F32) * own_key, axis=1, keepdims=True)
        own = jnp.where(lane == j, score * (HD ** -0.5), own)

    def peaks(u, top):
        p = turn(pair - u)
        z2_in(p).wait_recv()
        return jnp.maximum(top, zm[p, :, width:])

    my_stat = mixb[me, :, width:]
    top = lax.fori_loop(1, pairs, peaks, jnp.maximum(own, my_stat))
    own_weight = jnp.exp(own - top)
    scale = jnp.exp(my_stat - top)
    for j in range(local):
        at = slice(j * HD, (j + 1) * HD)
        hacc[:, at] = own_weight[:, j:j + 1] * own_value + scale[:, j:j + 1] * mixb[me, :, at]

    def add(u, total):
        p = turn(pair - u)
        stat = zm[p, :, width:]
        scale = jnp.exp(stat - top)
        for j in range(local):
            at = slice(j * HD, (j + 1) * HD)
            hacc[:, at] = hacc[:, at] + scale[:, j:j + 1] * zm[p, :, at]
        return total + scale * pltpu.roll(stat, half, 1)

    total = lax.fori_loop(1, pairs, add, own_weight + scale * pltpu.roll(my_stat, half, 1))
    for j in range(local):
        at = slice(j * HD, (j + 1) * HD)
        hg[me, :, at] = (hacc[:, at] / total[:, j:j + 1]).astype(BF16)

    spread2 = Spread(hg, hss, hsr, hys, hyr, hzs, hzr)
    spread2.begin()

    def product(d):
        load_wo(d).wait()
        acc[...] = acc[...] + jnp.dot(hg[d], wbuf[d], preferred_element_type=F32)

    acc[...] = jnp.zeros_like(acc)
    product(me)
    spread2.relay_far(pair)
    spread2.from_sibling(chip).wait_recv()
    product(sibling)

    def project_out(p):
        spread2.relay_near(p)
        before = turn(p + 1)
        product(2 * far(before) + core)
        spread2.from_sibling(far(before)).wait_recv()
        product(2 * far(before) + other)
        spread2.relay_far(p)
        product(along(p))
        spread2.from_sibling(near(p)).wait_recv()
        product(2 * near(p) + other)

    each_other(project_out)
    last = turn(pair + 1)
    product(2 * far(last) + core)
    spread2.from_sibling(far(last)).wait_recv()
    product(2 * far(last) + other)
    out[...] = acc[...].astype(BF16)

    def drain_chip(c, carry):
        sib1(c).wait_send()
        sib2(c).wait_send()
        spread1.to_sibling(c).wait_send()
        spread2.to_sibling(c).wait_send()
        return carry

    def drain_pair(p, carry):
        y1(p).wait_send()
        y2(p).wait_send()
        spread1.to_across(p).wait_send()
        spread2.to_across(p).wait_send()
        return carry

    def drain_along(p):
        z1(p).wait_send()
        z2(p).wait_send()
        spread1.to_along(p).wait_send()
        spread2.to_along(p).wait_send()

    lax.fori_loop(0, chips, drain_chip, 0)
    lax.fori_loop(0, pairs, drain_pair, 0)
    each_other(drain_along)


def on_device(hidden, norm_gain, w_query, w_key, w_value, w_out, cache_keys, cache_values, lengths):
    n = lax.axis_size("gx")
    rows, depth = hidden.shape
    spots, kv_width = cache_keys.shape[1:]
    width = w_query.shape[1] // n
    out_width = w_out.shape[1]
    chips = n // 2
    pairs = chips // 2
    vmem = pl.BlockSpec(memory_space=pltpu.VMEM)
    hbm = pl.BlockSpec(memory_space=pl.ANY)
    dma = pltpu.SemaphoreType.DMA
    return pl.pallas_call(
        functools.partial(kernel, n),
        out_shape=(
            jax.ShapeDtypeStruct((rows, out_width), BF16),
            jax.ShapeDtypeStruct((2, rows, kv_width), BF16),
        ),
        in_specs=[vmem, vmem, pl.BlockSpec(memory_space=pltpu.SMEM)] + [hbm] * 6,
        out_specs=(vmem, vmem),
        scratch_shapes=[
            pltpu.VMEM((n, depth, width), BF16),
            pltpu.VMEM((2, depth, kv_width), BF16),
            pltpu.VMEM((rows * spots, kv_width), BF16),
            pltpu.VMEM((rows * spots, kv_width), BF16),
            pltpu.VMEM((rows, 2 * kv_width), F32),
            pltpu.VMEM((n, rows, width + 2 * HD), F32),
            pltpu.VMEM((chips, rows, width + 2 * HD), F32),
            pltpu.VMEM((pairs, rows, width + 2 * HD), F32),
            pltpu.VMEM((pairs, rows, width + 2 * HD), F32),
            pltpu.VMEM((n, rows, width + HD), BF16),
            pltpu.VMEM((n, rows, width + HD), F32),
            pltpu.VMEM((chips, rows, width + HD), F32),
            pltpu.VMEM((pairs, rows, width + HD), F32),
            pltpu.VMEM((pairs, rows, width + HD), F32),
            pltpu.VMEM((rows, width), F32),
            pltpu.VMEM((n, rows, width), BF16),
            pltpu.VMEM((rows, out_width), F32),
            dma((n,)), dma((2,)), dma((n,)), dma((2,)),
        ] + [dma((size,)) for size in (chips, chips, pairs, pairs, pairs, pairs) * 4],
        compiler_params=pltpu.CompilerParams(
            collective_id=0, has_side_effects=True, vmem_limit_bytes=60 * 1024 * 1024),
        cost_estimate=pl.CostEstimate(
            flops=4 * rows * depth * n * width, bytes_accessed=4 * depth * n * width, transcendentals=0),
    )(
        hidden, norm_gain, lengths, w_query, w_key, w_value, w_out,
        cache_keys.reshape(rows * spots, kv_width), cache_values.reshape(rows * spots, kv_width),
    )


def solution(mesh):
    return jax.shard_map(
        on_device,
        mesh=mesh,
        in_specs=(
            P("grp", "gx"),
            P("gx"),
            P("gx", None),
            P("gx", None),
            P("gx", None),
            P(None, "gx"),
            P("grp", "gx", None),
            P("grp", "gx", None),
            P("grp"),
        ),
        out_specs=(P("grp", "gx"), P(None, "grp", None)),
        check_vma=False,
    )
```

```python
import functools
import math

import jax
import jax.numpy as jnp
from jax import lax
from jax.experimental import pallas as pl
from jax.experimental.pallas import tpu as pltpu
from jax.sharding import PartitionSpec as P

HD = 128
EPS = 1e-05
BASE = 500000.0
AHEAD = 8
F32 = jnp.float32
BF16 = jnp.bfloat16


def kernel(
    n, hidden, gain, lengths, wq, wk, wv, wo, ck, cv,
    out, new,
    wbuf, kvbuf, ckb, cvb, kvp, part, sibr, yr, zr, qg, mixb, sibm, ym, zm, hacc, hg, acc,
    wsem, kvsem, wosem, csem, s1s, s1r, y1s, y1r, z1s, z1r, gss, gsr, gds, gdr,
    s2s, s2r, y2s, y2r, z2s, z2r, hss, hsr, hds, hdr,
):
    rows, depth = hidden.shape
    width = wbuf.shape[2]
    local = width // HD
    kv = ck.shape[1] // HD
    group = n * local // kv
    chips = n // 2
    pairs = chips // 2
    per_kv = group // local
    chips_kv = per_kv // 2
    kv_devs = n // (2 * kv)
    spots = ck.shape[0] // rows
    half = HD // 2
    me = lax.axis_index("gx")
    core = lax.rem(me, 2)
    chip = me // 2
    side = lax.rem(chip, 2)
    pair = chip // 2
    other = 1 - core
    sibling = 2 * chip + other
    across = 2 * (2 * pair + 1 - side) + core

    def turn(index):
        return lax.rem(index + 2 * pairs, pairs)

    def near(p):
        return 2 * p + side

    def far(p):
        return 2 * p + 1 - side

    def along(p):
        return 2 * near(p) + core

    def remote(src, dst, send, recv, target):
        return pltpu.make_async_remote_copy(
            src_ref=src, dst_ref=dst, send_sem=send, recv_sem=recv,
            device_id={"gx": target}, device_id_type=pl.DeviceIdType.MESH,
        )

    def each_other(body):
        def step(u, carry):
            body(turn(pair - u))
            return carry
        lax.fori_loop(1, pairs, step, 0)

    barrier = pltpu.get_barrier_semaphore()

    def greet(target):
        pl.semaphore_signal(barrier, inc=1, device_id={"gx": target}, device_id_type=pl.DeviceIdType.MESH)

    greet(sibling)

    def greet_chip(u, carry):
        greet(2 * lax.rem(chip + u, chips) + core)
        return carry

    lax.fori_loop(1, chips, greet_chip, 0)

    def block(t, second):
        c = 2 * turn(pair + 1 + t) + lax.rem(side + 1 + t // pairs, 2)
        return c, 2 * c + (core if second else other)

    def load_w(t, second):
        d = block(t, second)[1]
        return pltpu.make_async_copy(
            wq.at[:, pl.ds(pl.multiple_of(d * width, HD), width)], wbuf.at[d], wsem.at[d])

    copy_k = pltpu.make_async_copy(wk, kvbuf.at[0], kvsem.at[0])
    copy_v = pltpu.make_async_copy(wv, kvbuf.at[1], kvsem.at[1])
    copy_k.start()
    copy_v.start()
    for t in range(AHEAD // 2):
        load_w(t, 0).start()
        load_w(t, 1).start()

    row_at = lax.broadcasted_iota(jnp.int32, (rows, HD), 0)
    lane = lax.broadcasted_iota(jnp.int32, (rows, HD), 1)
    owner_row = lax.broadcasted_iota(jnp.int32, (1, rows * spots), 1)
    by_row = jnp.zeros((rows, HD), jnp.int32)
    by_column = jnp.zeros((1, rows * spots), jnp.int32)
    for r in range(rows):
        size = lengths[r]
        by_row = jnp.where(row_at == r, size, by_row)
        by_column = jnp.where(owner_row // spots == r, size, by_column)
    limit = by_column - lax.rem(owner_row, spots)
    frequency = jnp.exp(lax.rem(lane, half).astype(F32) * (-2.0 * math.log(BASE) / HD))
    angles = by_row.astype(F32) * frequency
    cos_table = jnp.cos(angles)
    sin_table = jnp.sin(angles)
    sin_table = jnp.where(lane < half, -sin_table, sin_table)

    wide = hidden[...].astype(F32)
    squares = jnp.broadcast_to(jnp.sum(wide * wide, axis=1, keepdims=True), (rows, HD))
    scaled = (wide * gain[...].astype(F32)[None, :]).astype(BF16)
    kv_width = kv * HD
    copy_k.wait()
    kvp[:, :kv_width] = jnp.dot(scaled, kvbuf[0], preferred_element_type=F32)
    copy_v.wait()
    kvp[:, kv_width:] = jnp.dot(scaled, kvbuf[1], preferred_element_type=F32)

    pl.semaphore_wait(barrier, chips)

    def sib1(c):
        return remote(part.at[2 * c + other], sibr.at[c], s1s.at[c], s1r.at[c], sibling)

    def y1(p):
        return remote(part.at[2 * far(p) + core], yr.at[p], y1s.at[p], y1r.at[p], across)

    def z1(p):
        return remote(part.at[along(p)], zr.at[pair], z1s.at[p], z1r.at[pair], along(p))

    def z1_in(p):
        return remote(part.at[me], zr.at[p], z1s.at[p], z1r.at[p], along(p))

    def finish1_far(p):
        c = far(p)
        sib1(c).wait_recv()
        part[2 * c + core] = part[2 * c + core] + sibr[c]
        y1(p).start()

    def finish1_near(p):
        c = near(p)
        sib1(c).wait_recv()
        y1(p).wait_recv()
        part[2 * c + core] = part[2 * c + core] + sibr[c] + yr[p]

    def project_chip(t):
        for second in range(2):
            c, d = block(t, second)
            load_w(t, second).wait()
            part[d, :, :width] = jnp.dot(scaled, wbuf[d], preferred_element_type=F32)
            start = pl.multiple_of((d // kv_devs) * HD, HD)
            part[d, :, width:width + HD] = kvp[:, pl.ds(start, HD)]
            part[d, :, width + HD:] = squares

            @pl.when(t + AHEAD // 2 < chips)
            def _():
                load_w(t + AHEAD // 2, second).start()

            if not second:
                sib1(c).start()

    def project_far(i, carry):
        project_chip(i)

        @pl.when(i > 0)
        def _():
            finish1_far(turn(pair + i))

        return carry

    def project_near(i, carry):
        project_chip(pairs + i)

        @pl.when(i == 0)
        def _():
            finish1_far(pair)

        @pl.when(i > 0)
        def _():
            before = turn(pair + i)
            finish1_near(before)
            z1(before).start()

        return carry

    lax.fori_loop(0, pairs, project_far, 0)
    lax.fori_loop(0, pairs, project_near, 0)

    copy_ck = pltpu.make_async_copy(ck, ckb, csem.at[0])
    copy_cv = pltpu.make_async_copy(cv, cvb, csem.at[1])
    copy_ck.start()
    copy_cv.start()

    def load_wo(d):
        return pltpu.make_async_copy(
            wo.at[pl.ds(pl.multiple_of(d * width, HD), width), :], wbuf.at[d], wosem.at[d])

    def start_wo(i, carry):
        p = turn(pair - i)
        for c in (near(p), far(p)):
            load_wo(2 * c + core).start()
            load_wo(2 * c + other).start()
        return carry

    lax.fori_loop(0, pairs, start_wo, 0)

    finish1_near(pair)

    def gather1(p):
        z1_in(p).wait_recv()
        part[me] = part[me] + zr[p]

    each_other(gather1)

    inv = lax.rsqrt(part[me, :, width + HD:] / (depth * n) + EPS)
    for j in range(local):
        x = part[me, :, j * HD:(j + 1) * HD] * inv
        qg[me, :, j * HD:(j + 1) * HD] = (x * cos_table + pltpu.roll(x, half, 1) * sin_table).astype(BF16)
    is_key = (me // kv_devs < kv).astype(F32)
    x = part[me, :, width:width + HD] * inv
    cos_key = cos_table * is_key + (1.0 - is_key)
    qg[me, :, width:] = (x * cos_key + pltpu.roll(x, half, 1) * (sin_table * is_key)).astype(BF16)

    class Spread:
        def __init__(self, ref, ss, sr, ds, dr):
            self.ref, self.ss, self.sr, self.ds, self.dr = ref, ss, sr, ds, dr

        def to_sibling(self, c):
            at = self.ref.at[2 * c + core]
            return remote(at, at, self.ss.at[c], self.sr.at[c], sibling)

        def from_sibling(self, c):
            at = self.ref.at[2 * c + other]
            return remote(at, at, self.ss.at[c], self.sr.at[c], sibling)

        def to_chip(self, c):
            at = self.ref.at[me]
            return remote(at, at, self.ds.at[c], self.dr.at[chip], 2 * c + core)

        def from_chip(self, c):
            at = self.ref.at[2 * c + core]
            return remote(at, at, self.ds.at[c], self.dr.at[c], 2 * c + core)

        def begin(self):
            self.to_sibling(chip).start()

            def send_far(u, carry):
                self.to_chip(far(turn(pair + u))).start()
                return carry

            def send_near(u, carry):
                self.to_chip(near(turn(pair + u))).start()
                return carry

            lax.fori_loop(0, pairs, send_far, 0)
            lax.fori_loop(1, pairs, send_near, 0)

        def relay(self, c):
            self.from_chip(c).wait_recv()
            self.to_sibling(c).start()

    spread1 = Spread(qg, gss, gsr, gds, gdr)
    spread1.begin()

    column = lax.broadcasted_iota(jnp.int32, (group * rows, rows * spots), 1)
    row = lax.broadcasted_iota(jnp.int32, (group * rows, rows * spots), 0)
    valid = (lax.rem(row, rows) == column // spots) & (limit > me * spots)

    def sib2(c):
        return remote(mixb.at[2 * c + other], sibm.at[c], s2s.at[c], s2r.at[c], sibling)

    def y2(p):
        return remote(mixb.at[2 * far(p) + core], ym.at[p], y2s.at[p], y2r.at[p], across)

    def z2(p):
        return remote(mixb.at[along(p)], zm.at[pair], z2s.at[p], z2r.at[pair], along(p))

    def z2_in(p):
        return remote(mixb.at[me], zm.at[p], z2s.at[p], z2r.at[p], along(p))

    def merge(d, from_ref, index):
        first, second = mixb[d, :, width:], from_ref[index, :, width:]
        top = jnp.maximum(first, second)
        e_first, e_second = jnp.exp(first - top), jnp.exp(second - top)
        total = pltpu.roll(first, half, 1) * e_first + pltpu.roll(second, half, 1) * e_second
        mixb[d, :, width:] = jnp.where(lane < half, top, pltpu.roll(total, half, 1))
        for j in range(local):
            at = slice(j * HD, (j + 1) * HD)
            mixb[d, :, at] = e_first[:, j:j + 1] * mixb[d, :, at] + e_second[:, j:j + 1] * from_ref[index, :, at]

    def finish2_far(p):
        c = far(p)
        sib2(c).wait_recv()
        merge(2 * c + core, sibm, c)
        y2(p).start()

    def finish2_near(p):
        c = near(p)
        sib2(c).wait_recv()
        merge(2 * c + core, sibm, c)
        y2(p).wait_recv()
        merge(2 * c + core, ym, p)

        @pl.when(p != pair)
        def _():
            z2(p).start()

    def attend(k):
        query = jnp.concatenate(
            [qg[k * per_kv + h // local, :, (h % local) * HD:(h % local + 1) * HD] for h in range(group)], axis=0)
        at = pl.ds(pl.multiple_of(k * HD, HD), HD)
        scores = lax.dot_general(
            query, ckb[:, at], (((1,), (1,)), ((), ())), preferred_element_type=F32) * (HD ** -0.5)
        scores = jnp.where(valid, scores, -1e30)
        peak = jnp.max(scores, axis=1, keepdims=True)
        weights = jnp.where(valid, jnp.exp(scores - peak), 0.0)
        total = jnp.sum(weights, axis=1, keepdims=True)
        mix = jnp.dot(weights.astype(BF16), cvb[:, at], preferred_element_type=F32)
        for i in range(per_kv):
            d = k * per_kv + i
            stat = jnp.zeros((rows, HD), F32)
            for j in range(local):
                h = i * local + j
                here = slice(h * rows, (h + 1) * rows)
                mixb[d, :, j * HD:(j + 1) * HD] = mix[here]
                stat = jnp.where(lane == j, peak[here], stat)
                stat = jnp.where(lane == half + j, total[here], stat)
            mixb[d, :, width:] = stat

        def send(i, carry):
            sib2(k * chips_kv + i).start()
            return carry

        lax.fori_loop(0, chips_kv, send, 0)

    if chips_kv == 1:
        copy_ck.wait()
        copy_cv.wait()
        spread1.from_sibling(chip).wait_recv()
        attend(chip)
        spread1.relay(far(pair))

        def attend_far(u, carry):
            p = turn(pair - u)

            @pl.when(u + 1 < pairs)
            def _():
                spread1.relay(far(turn(pair - u - 1)))

            @pl.when(u + 1 == pairs)
            def _():
                spread1.relay(near(turn(pair - 1)))

            spread1.from_sibling(far(p)).wait_recv()
            attend(far(p))

            @pl.when(u > 0)
            def _():
                finish2_far(turn(p + 1))

            return carry

        def attend_near(u, carry):
            p = turn(pair - u)

            @pl.when(u + 1 < pairs)
            def _():
                spread1.relay(near(turn(pair - u - 1)))

            spread1.from_sibling(near(p)).wait_recv()
            attend(near(p))

            @pl.when(u == 1)
            def _():
                finish2_far(turn(pair + 1))

            @pl.when(u > 1)
            def _():
                finish2_near(turn(p + 1))

            return carry

        lax.fori_loop(0, pairs, attend_far, 0)
        lax.fori_loop(1, pairs, attend_near, 0)
        finish2_near(turn(pair + 1))
        finish2_near(pair)
    else:
        spread1.relay(far(pair))
        each_other(lambda p: spread1.relay(far(p)))
        each_other(lambda p: spread1.relay(near(p)))
        copy_ck.wait()
        copy_cv.wait()

        def wait_chip(c, carry):
            spread1.from_sibling(c).wait_recv()
            return carry

        lax.fori_loop(0, chips, wait_chip, 0)

        def of_kv(k, carry):
            attend(k)

            def finish_far(i, inner):
                finish2_far(k * chips_kv // 2 + i)
                return inner

            def finish_near(i, inner):
                finish2_near(k * chips_kv // 2 + i)
                return inner

            lax.fori_loop(0, chips_kv // 2, finish_far, 0)
            lax.fori_loop(0, chips_kv // 2, finish_near, 0)
            return carry

        lax.fori_loop(0, kv, of_kv, 0)

    for i in range(kv):
        new[0, :, i * HD:(i + 1) * HD] = qg[i * kv_devs, :, width:]
        new[1, :, i * HD:(i + 1) * HD] = qg[(kv + i) * kv_devs, :, width:]

    my_kv = me * local // group
    own_key = qg[my_kv * kv_devs, :, width:].astype(F32)
    own_value = qg[(kv + my_kv) * kv_devs, :, width:].astype(F32)
    own = jnp.zeros((rows, HD), F32)
    for j in range(local):
        score = jnp.sum(qg[me, :, j * HD:(j + 1) * HD].astype(F32) * own_key, axis=1, keepdims=True)
        own = jnp.where(lane == j, score * (HD ** -0.5), own)

    def peaks(u, top):
        p = turn(pair - u)
        z2_in(p).wait_recv()
        return jnp.maximum(top, zm[p, :, width:])

    my_stat = mixb[me, :, width:]
    top = lax.fori_loop(1, pairs, peaks, jnp.maximum(own, my_stat))
    own_weight = jnp.exp(own - top)
    scale = jnp.exp(my_stat - top)
    for j in range(local):
        at = slice(j * HD, (j + 1) * HD)
        hacc[:, at] = own_weight[:, j:j + 1] * own_value + scale[:, j:j + 1] * mixb[me, :, at]

    def add(u, total):
        p = turn(pair - u)
        stat = zm[p, :, width:]
        scale = jnp.exp(stat - top)
        for j in range(local):
            at = slice(j * HD, (j + 1) * HD)
            hacc[:, at] = hacc[:, at] + scale[:, j:j + 1] * zm[p, :, at]
        return total + scale * pltpu.roll(stat, half, 1)

    total = lax.fori_loop(1, pairs, add, own_weight + scale * pltpu.roll(my_stat, half, 1))
    for j in range(local):
        at = slice(j * HD, (j + 1) * HD)
        hg[me, :, at] = (hacc[:, at] / total[:, j:j + 1]).astype(BF16)

    spread2 = Spread(hg, hss, hsr, hds, hdr)
    spread2.begin()

    def product(d):
        load_wo(d).wait()
        acc[...] = acc[...] + jnp.dot(hg[d], wbuf[d], preferred_element_type=F32)

    acc[...] = jnp.zeros_like(acc)
    product(me)
    spread2.from_sibling(chip).wait_recv()
    product(sibling)

    def project_out(c, before, first):
        spread2.relay(c)
        if not first:
            spread2.from_sibling(before).wait_recv()
            product(2 * before + other)
        product(2 * c + core)

    def out_far(u, carry):
        p = turn(pair - u)
        project_out(far(p), far(turn(p + 1)), False)
        return carry

    def out_near(u, carry):
        p = turn(pair - u)
        project_out(near(p), near(turn(p + 1)), False)
        return carry

    project_out(far(pair), chip, True)
    lax.fori_loop(1, pairs, out_far, 0)
    last = far(turn(pair + 1))
    project_out(near(turn(pair - 1)), last, False)
    lax.fori_loop(2, pairs, out_near, 0)
    last = near(turn(pair + 1))
    spread2.from_sibling(last).wait_recv()
    product(2 * last + other)
    out[...] = acc[...].astype(BF16)

    def drain_chip(c, carry):
        sib1(c).wait_send()
        sib2(c).wait_send()
        spread1.to_sibling(c).wait_send()
        spread2.to_sibling(c).wait_send()
        return carry

    def drain_pair(p, carry):
        y1(p).wait_send()
        y2(p).wait_send()
        spread1.to_chip(far(p)).wait_send()
        spread2.to_chip(far(p)).wait_send()
        return carry

    def drain_along(p):
        z1(p).wait_send()
        z2(p).wait_send()
        spread1.to_chip(near(p)).wait_send()
        spread2.to_chip(near(p)).wait_send()

    lax.fori_loop(0, chips, drain_chip, 0)
    lax.fori_loop(0, pairs, drain_pair, 0)
    each_other(drain_along)


def on_device(hidden, norm_gain, w_query, w_key, w_value, w_out, cache_keys, cache_values, lengths):
    n = lax.axis_size("gx")
    rows, depth = hidden.shape
    spots, kv_width = cache_keys.shape[1:]
    width = w_query.shape[1] // n
    out_width = w_out.shape[1]
    chips = n // 2
    pairs = chips // 2
    vmem = pl.BlockSpec(memory_space=pltpu.VMEM)
    hbm = pl.BlockSpec(memory_space=pl.ANY)
    dma = pltpu.SemaphoreType.DMA
    return pl.pallas_call(
        functools.partial(kernel, n),
        out_shape=(
            jax.ShapeDtypeStruct((rows, out_width), BF16),
            jax.ShapeDtypeStruct((2, rows, kv_width), BF16),
        ),
        in_specs=[vmem, vmem, pl.BlockSpec(memory_space=pltpu.SMEM)] + [hbm] * 6,
        out_specs=(vmem, vmem),
        scratch_shapes=[
            pltpu.VMEM((n, depth, width), BF16),
            pltpu.VMEM((2, depth, kv_width), BF16),
            pltpu.VMEM((rows * spots, kv_width), BF16),
            pltpu.VMEM((rows * spots, kv_width), BF16),
            pltpu.VMEM((rows, 2 * kv_width), F32),
            pltpu.VMEM((n, rows, width + 2 * HD), F32),
            pltpu.VMEM((chips, rows, width + 2 * HD), F32),
            pltpu.VMEM((pairs, rows, width + 2 * HD), F32),
            pltpu.VMEM((pairs, rows, width + 2 * HD), F32),
            pltpu.VMEM((n, rows, width + HD), BF16),
            pltpu.VMEM((n, rows, width + HD), F32),
            pltpu.VMEM((chips, rows, width + HD), F32),
            pltpu.VMEM((pairs, rows, width + HD), F32),
            pltpu.VMEM((pairs, rows, width + HD), F32),
            pltpu.VMEM((rows, width), F32),
            pltpu.VMEM((n, rows, width), BF16),
            pltpu.VMEM((rows, out_width), F32),
            dma((n,)), dma((2,)), dma((n,)), dma((2,)),
        ] + [dma((size,)) for size in (chips, chips, pairs, pairs, pairs, pairs, chips, chips, chips, chips) * 2],
        compiler_params=pltpu.CompilerParams(
            collective_id=0, has_side_effects=True, vmem_limit_bytes=60 * 1024 * 1024),
        cost_estimate=pl.CostEstimate(
            flops=4 * rows * depth * n * width, bytes_accessed=4 * depth * n * width, transcendentals=0),
    )(
        hidden, norm_gain, lengths, w_query, w_key, w_value, w_out,
        cache_keys.reshape(rows * spots, kv_width), cache_values.reshape(rows * spots, kv_width),
    )


def solution(mesh):
    return jax.shard_map(
        on_device,
        mesh=mesh,
        in_specs=(
            P("grp", "gx"),
            P("gx"),
            P("gx", None),
            P("gx", None),
            P("gx", None),
            P(None, "gx"),
            P("grp", "gx", None),
            P("grp", "gx", None),
            P("grp"),
        ),
        out_specs=(P("grp", "gx"), P(None, "grp", None)),
        check_vma=False,
    )
```

```python
import functools
import math

import jax
import jax.numpy as jnp
from jax import lax
from jax.experimental import pallas as pl
from jax.experimental.pallas import tpu as pltpu
from jax.sharding import PartitionSpec as P

HD = 128
EPS = 1e-05
BASE = 500000.0
AHEAD = 8
F32 = jnp.float32
BF16 = jnp.bfloat16


def kernel(
    n, hidden, gain, lengths, wq, wk, wv, wo, ck, cv,
    out, new,
    wbuf, kvbuf, ckb, cvb, kvp, part, sibr, yr, zr, qg, mixb, sibm, ym, zm, hacc, hg, acc,
    wsem, kvsem, wosem, csem, s1s, s1r, y1s, y1r, z1s, z1r, gss, gsr, gds, gdr,
    s2s, s2r, y2s, y2r, z2s, z2r, hss, hsr, hds, hdr,
):
    rows, depth = hidden.shape
    width = wbuf.shape[2]
    local = width // HD
    kv = ck.shape[1] // HD
    group = n * local // kv
    chips = n // 2
    pairs = chips // 2
    per_kv = group // local
    chips_kv = per_kv // 2
    kv_devs = n // (2 * kv)
    spots = ck.shape[0] // rows
    half = HD // 2
    me = lax.axis_index("gx")
    core = lax.rem(me, 2)
    chip = me // 2
    side = lax.rem(chip, 2)
    pair = chip // 2
    other = 1 - core
    sibling = 2 * chip + other
    across = 2 * (2 * pair + 1 - side) + core

    def turn(index):
        return lax.rem(index + 2 * pairs, pairs)

    def near(p):
        return 2 * p + side

    def far(p):
        return 2 * p + 1 - side

    def along(p):
        return 2 * near(p) + core

    def remote(src, dst, send, recv, target):
        return pltpu.make_async_remote_copy(
            src_ref=src, dst_ref=dst, send_sem=send, recv_sem=recv,
            device_id={"gx": target}, device_id_type=pl.DeviceIdType.MESH,
        )

    def each_other(body):
        def step(u, carry):
            body(turn(pair - u))
            return carry
        lax.fori_loop(1, pairs, step, 0)

    barrier = pltpu.get_barrier_semaphore()

    def greet(target):
        pl.semaphore_signal(barrier, inc=1, device_id={"gx": target}, device_id_type=pl.DeviceIdType.MESH)

    greet(sibling)

    def greet_chip(u, carry):
        greet(2 * lax.rem(chip + u, chips) + core)
        return carry

    lax.fori_loop(1, chips, greet_chip, 0)

    def block(t, second):
        c = 2 * turn(pair + 1 + t) + lax.rem(side + 1 + t // pairs, 2)
        return c, 2 * c + (core if second else other)

    def load_w(t, second):
        d = block(t, second)[1]
        return pltpu.make_async_copy(
            wq.at[:, pl.ds(pl.multiple_of(d * width, HD), width)], wbuf.at[d], wsem.at[d])

    copy_k = pltpu.make_async_copy(wk, kvbuf.at[0], kvsem.at[0])
    copy_v = pltpu.make_async_copy(wv, kvbuf.at[1], kvsem.at[1])
    copy_k.start()
    copy_v.start()
    for t in range(AHEAD // 2):
        load_w(t, 0).start()
        load_w(t, 1).start()

    row_at = lax.broadcasted_iota(jnp.int32, (rows, HD), 0)
    lane = lax.broadcasted_iota(jnp.int32, (rows, HD), 1)
    owner_row = lax.broadcasted_iota(jnp.int32, (1, rows * spots), 1)
    by_row = jnp.zeros((rows, HD), jnp.int32)
    by_column = jnp.zeros((1, rows * spots), jnp.int32)
    for r in range(rows):
        size = lengths[r]
        by_row = jnp.where(row_at == r, size, by_row)
        by_column = jnp.where(owner_row // spots == r, size, by_column)
    limit = by_column - lax.rem(owner_row, spots)
    frequency = jnp.exp(lax.rem(lane, half).astype(F32) * (-2.0 * math.log(BASE) / HD))
    angles = by_row.astype(F32) * frequency
    cos_table = jnp.cos(angles)
    sin_table = jnp.sin(angles)
    sin_table = jnp.where(lane < half, -sin_table, sin_table)

    wide = hidden[...].astype(F32)
    squares = jnp.broadcast_to(jnp.sum(wide * wide, axis=1, keepdims=True), (rows, HD))
    scaled = (wide * gain[...].astype(F32)[None, :]).astype(BF16)
    kv_width = kv * HD
    copy_k.wait()
    kvp[:, :kv_width] = jnp.dot(scaled, kvbuf[0], preferred_element_type=F32)
    copy_v.wait()
    kvp[:, kv_width:] = jnp.dot(scaled, kvbuf[1], preferred_element_type=F32)

    pl.semaphore_wait(barrier, chips)

    def sib1(c):
        return remote(part.at[2 * c + other], sibr.at[c], s1s.at[c], s1r.at[c], sibling)

    def y1(p):
        return remote(part.at[2 * far(p) + core], yr.at[p], y1s.at[p], y1r.at[p], across)

    def z1(p):
        return remote(part.at[along(p)], zr.at[pair], z1s.at[p], z1r.at[pair], along(p))

    def z1_in(p):
        return remote(part.at[me], zr.at[p], z1s.at[p], z1r.at[p], along(p))

    def finish1_far(p):
        c = far(p)
        sib1(c).wait_recv()
        part[2 * c + core] = part[2 * c + core] + sibr[c]
        y1(p).start()

    def finish1_near(p):
        c = near(p)
        sib1(c).wait_recv()
        y1(p).wait_recv()
        part[2 * c + core] = part[2 * c + core] + sibr[c] + yr[p]

    def project_chip(t, between):
        for second in range(2):
            c, d = block(t, second)
            load_w(t, second).wait()
            part[d, :, :width] = jnp.dot(scaled, wbuf[d], preferred_element_type=F32)
            start = pl.multiple_of((d // kv_devs) * HD, HD)
            part[d, :, width:width + HD] = kvp[:, pl.ds(start, HD)]
            part[d, :, width + HD:] = squares

            @pl.when(t + AHEAD // 2 < chips)
            def _():
                load_w(t + AHEAD // 2, second).start()

            if not second:
                sib1(c).start()
                between()

    def project_far(i, carry):
        def between():
            @pl.when(i > 0)
            def _():
                finish1_far(turn(pair + i))

        project_chip(i, between)
        return carry

    def project_near(i, carry):
        def between():
            @pl.when(i == 0)
            def _():
                finish1_far(pair)

            @pl.when(i > 0)
            def _():
                before = turn(pair + i)
                finish1_near(before)
                z1(before).start()

        project_chip(pairs + i, between)
        return carry

    lax.fori_loop(0, pairs, project_far, 0)
    lax.fori_loop(0, pairs, project_near, 0)

    copy_ck = pltpu.make_async_copy(ck, ckb, csem.at[0])
    copy_cv = pltpu.make_async_copy(cv, cvb, csem.at[1])
    copy_ck.start()
    copy_cv.start()

    def load_wo(d):
        return pltpu.make_async_copy(
            wo.at[pl.ds(pl.multiple_of(d * width, HD), width), :], wbuf.at[d], wosem.at[d])

    def start_wo(i, carry):
        p = turn(pair - i)
        for c in (near(p), far(p)):
            load_wo(2 * c + core).start()
            load_wo(2 * c + other).start()
        return carry

    lax.fori_loop(0, pairs, start_wo, 0)

    finish1_near(pair)

    def gather1(p):
        z1_in(p).wait_recv()
        part[me] = part[me] + zr[p]

    each_other(gather1)

    inv = lax.rsqrt(part[me, :, width + HD:] / (depth * n) + EPS)
    for j in range(local):
        x = part[me, :, j * HD:(j + 1) * HD] * inv
        qg[me, :, j * HD:(j + 1) * HD] = (x * cos_table + pltpu.roll(x, half, 1) * sin_table).astype(BF16)
    is_key = (me // kv_devs < kv).astype(F32)
    x = part[me, :, width:width + HD] * inv
    cos_key = cos_table * is_key + (1.0 - is_key)
    qg[me, :, width:] = (x * cos_key + pltpu.roll(x, half, 1) * (sin_table * is_key)).astype(BF16)

    class Spread:
        def __init__(self, ref, ss, sr, ds, dr):
            self.ref, self.ss, self.sr, self.ds, self.dr = ref, ss, sr, ds, dr

        def to_sibling(self, c):
            at = self.ref.at[2 * c + core]
            return remote(at, at, self.ss.at[c], self.sr.at[c], sibling)

        def from_sibling(self, c):
            at = self.ref.at[2 * c + other]
            return remote(at, at, self.ss.at[c], self.sr.at[c], sibling)

        def to_chip(self, c):
            at = self.ref.at[me]
            return remote(at, at, self.ds.at[c], self.dr.at[chip], 2 * c + core)

        def from_chip(self, c):
            at = self.ref.at[2 * c + core]
            return remote(at, at, self.ds.at[c], self.dr.at[c], 2 * c + core)

        def begin(self):
            self.to_sibling(chip).start()

            def send_far(u, carry):
                self.to_chip(far(turn(pair + u))).start()
                return carry

            def send_near(u, carry):
                self.to_chip(near(turn(pair + u))).start()
                return carry

            lax.fori_loop(0, pairs, send_far, 0)
            lax.fori_loop(1, pairs, send_near, 0)

        def relay(self, c):
            self.from_chip(c).wait_recv()
            self.to_sibling(c).start()

    spread1 = Spread(qg, gss, gsr, gds, gdr)
    spread1.begin()

    column = lax.broadcasted_iota(jnp.int32, (group * rows, rows * spots), 1)
    row = lax.broadcasted_iota(jnp.int32, (group * rows, rows * spots), 0)
    valid = (lax.rem(row, rows) == column // spots) & (limit > me * spots)

    def sib2(c):
        return remote(mixb.at[2 * c + other], sibm.at[c], s2s.at[c], s2r.at[c], sibling)

    def y2(p):
        return remote(mixb.at[2 * far(p) + core], ym.at[p], y2s.at[p], y2r.at[p], across)

    def z2(p):
        return remote(mixb.at[along(p)], zm.at[pair], z2s.at[p], z2r.at[pair], along(p))

    def z2_in(p):
        return remote(mixb.at[me], zm.at[p], z2s.at[p], z2r.at[p], along(p))

    def merge(d, from_ref, index):
        first, second = mixb[d, :, width:], from_ref[index, :, width:]
        top = jnp.maximum(first, second)
        e_first, e_second = jnp.exp(first - top), jnp.exp(second - top)
        total = pltpu.roll(first, half, 1) * e_first + pltpu.roll(second, half, 1) * e_second
        mixb[d, :, width:] = jnp.where(lane < half, top, pltpu.roll(total, half, 1))
        for j in range(local):
            at = slice(j * HD, (j + 1) * HD)
            mixb[d, :, at] = e_first[:, j:j + 1] * mixb[d, :, at] + e_second[:, j:j + 1] * from_ref[index, :, at]

    def finish2_far(p):
        c = far(p)
        sib2(c).wait_recv()
        merge(2 * c + core, sibm, c)
        y2(p).start()

    def finish2_near(p):
        c = near(p)
        sib2(c).wait_recv()
        merge(2 * c + core, sibm, c)
        y2(p).wait_recv()
        merge(2 * c + core, ym, p)

        @pl.when(p != pair)
        def _():
            z2(p).start()

    def attend(k):
        query = jnp.concatenate(
            [qg[k * per_kv + h // local, :, (h % local) * HD:(h % local + 1) * HD] for h in range(group)], axis=0)
        at = pl.ds(pl.multiple_of(k * HD, HD), HD)
        scores = lax.dot_general(
            query, ckb[:, at], (((1,), (1,)), ((), ())), preferred_element_type=F32) * (HD ** -0.5)
        scores = jnp.where(valid, scores, -1e30)
        peak = jnp.max(scores, axis=1, keepdims=True)
        weights = jnp.where(valid, jnp.exp(scores - peak), 0.0)
        total = jnp.sum(weights, axis=1, keepdims=True)
        mix = jnp.dot(weights.astype(BF16), cvb[:, at], preferred_element_type=F32)
        for i in range(per_kv):
            d = k * per_kv + i
            stat = jnp.zeros((rows, HD), F32)
            for j in range(local):
                h = i * local + j
                here = slice(h * rows, (h + 1) * rows)
                mixb[d, :, j * HD:(j + 1) * HD] = mix[here]
                stat = jnp.where(lane == j, peak[here], stat)
                stat = jnp.where(lane == half + j, total[here], stat)
            mixb[d, :, width:] = stat

        def send(i, carry):
            sib2(k * chips_kv + i).start()
            return carry

        lax.fori_loop(0, chips_kv, send, 0)

    if chips_kv == 1:
        copy_ck.wait()
        copy_cv.wait()
        spread1.from_sibling(chip).wait_recv()
        attend(chip)
        spread1.relay(far(pair))

        def attend_far(u, carry):
            p = turn(pair - u)

            @pl.when(u + 1 < pairs)
            def _():
                spread1.relay(far(turn(pair - u - 1)))

            @pl.when(u + 1 == pairs)
            def _():
                spread1.relay(near(turn(pair - 1)))

            spread1.from_sibling(far(p)).wait_recv()
            attend(far(p))

            @pl.when(u > 0)
            def _():
                finish2_far(turn(p + 1))

            return carry

        def attend_near(u, carry):
            p = turn(pair - u)

            @pl.when(u + 1 < pairs)
            def _():
                spread1.relay(near(turn(pair - u - 1)))

            spread1.from_sibling(near(p)).wait_recv()
            attend(near(p))

            @pl.when(u == 1)
            def _():
                finish2_far(turn(pair + 1))

            @pl.when(u > 1)
            def _():
                finish2_near(turn(p + 1))

            return carry

        lax.fori_loop(0, pairs, attend_far, 0)
        lax.fori_loop(1, pairs, attend_near, 0)
        finish2_near(turn(pair + 1))
        finish2_near(pair)
    else:
        spread1.relay(far(pair))
        each_other(lambda p: spread1.relay(far(p)))
        each_other(lambda p: spread1.relay(near(p)))
        copy_ck.wait()
        copy_cv.wait()

        def wait_chip(c, carry):
            spread1.from_sibling(c).wait_recv()
            return carry

        lax.fori_loop(0, chips, wait_chip, 0)

        def of_kv(k, carry):
            attend(k)

            def finish_far(i, inner):
                finish2_far(k * chips_kv // 2 + i)
                return inner

            def finish_near(i, inner):
                finish2_near(k * chips_kv // 2 + i)
                return inner

            lax.fori_loop(0, chips_kv // 2, finish_far, 0)
            lax.fori_loop(0, chips_kv // 2, finish_near, 0)
            return carry

        lax.fori_loop(0, kv, of_kv, 0)

    for i in range(kv):
        new[0, :, i * HD:(i + 1) * HD] = qg[i * kv_devs, :, width:]
        new[1, :, i * HD:(i + 1) * HD] = qg[(kv + i) * kv_devs, :, width:]

    my_kv = me * local // group
    own_key = qg[my_kv * kv_devs, :, width:].astype(F32)
    own_value = qg[(kv + my_kv) * kv_devs, :, width:].astype(F32)
    own = jnp.zeros((rows, HD), F32)
    for j in range(local):
        score = jnp.sum(qg[me, :, j * HD:(j + 1) * HD].astype(F32) * own_key, axis=1, keepdims=True)
        own = jnp.where(lane == j, score * (HD ** -0.5), own)

    def peaks(u, top):
        p = turn(pair - u)
        z2_in(p).wait_recv()
        return jnp.maximum(top, zm[p, :, width:])

    my_stat = mixb[me, :, width:]
    top = lax.fori_loop(1, pairs, peaks, jnp.maximum(own, my_stat))
    own_weight = jnp.exp(own - top)
    scale = jnp.exp(my_stat - top)
    for j in range(local):
        at = slice(j * HD, (j + 1) * HD)
        hacc[:, at] = own_weight[:, j:j + 1] * own_value + scale[:, j:j + 1] * mixb[me, :, at]

    def add(u, total):
        p = turn(pair - u)
        stat = zm[p, :, width:]
        scale = jnp.exp(stat - top)
        for j in range(local):
            at = slice(j * HD, (j + 1) * HD)
            hacc[:, at] = hacc[:, at] + scale[:, j:j + 1] * zm[p, :, at]
        return total + scale * pltpu.roll(stat, half, 1)

    total = lax.fori_loop(1, pairs, add, own_weight + scale * pltpu.roll(my_stat, half, 1))
    for j in range(local):
        at = slice(j * HD, (j + 1) * HD)
        hg[me, :, at] = (hacc[:, at] / total[:, j:j + 1]).astype(BF16)

    spread2 = Spread(hg, hss, hsr, hds, hdr)
    spread2.begin()

    def product(d):
        load_wo(d).wait()
        acc[...] = acc[...] + jnp.dot(hg[d], wbuf[d], preferred_element_type=F32)

    acc[...] = jnp.zeros_like(acc)
    product(me)
    spread2.from_sibling(chip).wait_recv()
    product(sibling)

    def project_out(c, before, first):
        spread2.relay(c)
        if not first:
            spread2.from_sibling(before).wait_recv()
            product(2 * before + other)
        product(2 * c + core)

    def out_far(u, carry):
        p = turn(pair - u)
        project_out(far(p), far(turn(p + 1)), False)
        return carry

    def out_near(u, carry):
        p = turn(pair - u)
        project_out(near(p), near(turn(p + 1)), False)
        return carry

    project_out(far(pair), chip, True)
    lax.fori_loop(1, pairs, out_far, 0)
    last = far(turn(pair + 1))
    project_out(near(turn(pair - 1)), last, False)
    lax.fori_loop(2, pairs, out_near, 0)
    last = near(turn(pair + 1))
    spread2.from_sibling(last).wait_recv()
    product(2 * last + other)
    out[...] = acc[...].astype(BF16)

    def drain_chip(c, carry):
        sib1(c).wait_send()
        sib2(c).wait_send()
        spread1.to_sibling(c).wait_send()
        spread2.to_sibling(c).wait_send()
        return carry

    def drain_pair(p, carry):
        y1(p).wait_send()
        y2(p).wait_send()
        spread1.to_chip(far(p)).wait_send()
        spread2.to_chip(far(p)).wait_send()
        return carry

    def drain_along(p):
        z1(p).wait_send()
        z2(p).wait_send()
        spread1.to_chip(near(p)).wait_send()
        spread2.to_chip(near(p)).wait_send()

    lax.fori_loop(0, chips, drain_chip, 0)
    lax.fori_loop(0, pairs, drain_pair, 0)
    each_other(drain_along)


def place(first, second, first_out, second_out, sem):
    copies = [
        pltpu.make_async_copy(first, first_out, sem.at[0]),
        pltpu.make_async_copy(second, second_out, sem.at[1]),
    ]
    for copy in copies:
        copy.start()
    for copy in copies:
        copy.wait()


def on_device(hidden, norm_gain, w_query, w_key, w_value, w_out, cache_keys, cache_values, lengths):
    n = lax.axis_size("gx")
    rows, depth = hidden.shape
    spots, kv_width = cache_keys.shape[1:]
    width = w_query.shape[1] // n
    out_width = w_out.shape[1]
    chips = n // 2
    pairs = chips // 2
    vmem = pl.BlockSpec(memory_space=pltpu.VMEM)
    hbm = pl.BlockSpec(memory_space=pl.ANY)
    dma = pltpu.SemaphoreType.DMA
    results = pl.pallas_call(
        functools.partial(kernel, n),
        out_shape=(
            jax.ShapeDtypeStruct((rows, out_width), BF16),
            jax.ShapeDtypeStruct((2, rows, kv_width), BF16),
        ),
        in_specs=[vmem, vmem, pl.BlockSpec(memory_space=pltpu.SMEM)] + [hbm] * 6,
        out_specs=(vmem, vmem),
        scratch_shapes=[
            pltpu.VMEM((n, depth, width), BF16),
            pltpu.VMEM((2, depth, kv_width), BF16),
            pltpu.VMEM((rows * spots, kv_width), BF16),
            pltpu.VMEM((rows * spots, kv_width), BF16),
            pltpu.VMEM((rows, 2 * kv_width), F32),
            pltpu.VMEM((n, rows, width + 2 * HD), F32),
            pltpu.VMEM((chips, rows, width + 2 * HD), F32),
            pltpu.VMEM((pairs, rows, width + 2 * HD), F32),
            pltpu.VMEM((pairs, rows, width + 2 * HD), F32),
            pltpu.VMEM((n, rows, width + HD), BF16),
            pltpu.VMEM((n, rows, width + HD), F32),
            pltpu.VMEM((chips, rows, width + HD), F32),
            pltpu.VMEM((pairs, rows, width + HD), F32),
            pltpu.VMEM((pairs, rows, width + HD), F32),
            pltpu.VMEM((rows, width), F32),
            pltpu.VMEM((n, rows, width), BF16),
            pltpu.VMEM((rows, out_width), F32),
            dma((n,)), dma((2,)), dma((n,)), dma((2,)),
        ] + [dma((size,)) for size in (chips, chips, pairs, pairs, pairs, pairs, chips, chips, chips, chips) * 2],
        compiler_params=pltpu.CompilerParams(
            collective_id=0, has_side_effects=True, vmem_limit_bytes=60 * 1024 * 1024),
        cost_estimate=pl.CostEstimate(
            flops=4 * rows * depth * n * width, bytes_accessed=4 * depth * n * width, transcendentals=0),
    )(
        hidden, norm_gain, lengths, w_query, w_key, w_value, w_out,
        cache_keys.reshape(rows * spots, kv_width), cache_values.reshape(rows * spots, kv_width),
    )
    return pl.pallas_call(
        place,
        out_shape=tuple(jax.ShapeDtypeStruct(r.shape, r.dtype) for r in results),
        in_specs=[hbm] * 2,
        out_specs=(hbm, hbm),
        scratch_shapes=[dma((2,))],
        compiler_params=pltpu.CompilerParams(vmem_limit_bytes=60 * 1024 * 1024),
    )(*results)


def solution(mesh):
    return jax.shard_map(
        on_device,
        mesh=mesh,
        in_specs=(
            P("grp", "gx"),
            P("gx"),
            P("gx", None),
            P("gx", None),
            P("gx", None),
            P(None, "gx"),
            P("grp", "gx", None),
            P("grp", "gx", None),
            P("grp"),
        ),
        out_specs=(P("grp", "gx"), P(None, "grp", None)),
        check_vma=False,
    )
```
